128 devices in a mesh: section: 16 (over x_lo, z, core), seq: 8 (over y, x_hi).
Axes of the slice: x: 4 (x_hi: 2, x_lo: 2; x = x_hi * 2 + x_lo), y: 4, z: 4, core: 2. Of those that a mesh axis runs over, the one named last changes fastest.
Arguments:
- queries: bfloat16 [16, 1024, 8192], P('section', 'seq'), may hold values from -48 to 48
- key_states: bfloat16 [16, 1024, 1024], P('section', 'seq'), may hold values from -6 to 6
- section_value_states: bfloat16 [16, 1024, 1024], P('section', 'seq'), may hold values from -6 to 6
- out_grad: bfloat16 [16, 1024, 8192], P('section', 'seq'), may hold values from -1.5 to 1.5
- layer_input: bfloat16 [16, 1024, 8192], P('section', 'seq'), may hold values from -6 to 6
- doc_segments: int32 [16, 1024], P('section', 'seq'), may hold values from 0 to 3, never falling along the last dimension, each value on 1 to 512 neighbouring positions
Outputs:
- query_grad: bfloat16 [16, 1024, 8192], P('section', 'seq')
- key_grad: bfloat16 [16, 1024, 1024], P('section', 'seq')
- weight_grad: bfloat16 [16, 8192, 1024], P('section', None, 'seq')
The draws below stay inside these ranges and needn't reach their ends.
Inputs may be any that keep to these rules, and one draw needn't show every extreme that they name: `doc_segments`: document numbers never fall along a section's positions; a document holds at most 512 positions.
All inputs are finite; a program needn't handle non-finite values.
Results may differ from the reference program's by a relative error of at most 0.012.
The reference program's roundings to bfloat16 on the way count: a program that leaves them out, or rounds other values in their place, can miss the bound.
Values may be sent and summed in bfloat16 or wider, within the bound.
A program may use at most 128 MiB of HBM per device.

```python
import math
import jax
import jax.numpy as jnp
import numpy as np
from jax import lax

D = 8192
QUERY_HEADS = 64
KEY_VALUE_HEADS = 8
HEAD_WIDTH = 128
SECTION_LENGTH = 1024
RELAY_SECTIONS = 16


def drawn_pair(key):
    base = jax.random.fold_in(key, 11)
    key_sample, query_draw = jax.random.split(base, 2)
    key_entries = jnp.clip(jax.random.normal(key_sample, (RELAY_SECTIONS, SECTION_LENGTH, KEY_VALUE_HEADS, HEAD_WIDTH), jnp.float32), -6.0, 6.0)
    query_entries = jnp.clip(jax.random.normal(query_draw, (RELAY_SECTIONS, SECTION_LENGTH, QUERY_HEADS, HEAD_WIDTH), jnp.float32), -6.0, 6.0)
    return (query_entries.reshape(RELAY_SECTIONS, SECTION_LENGTH, QUERY_HEADS * HEAD_WIDTH), key_entries.reshape(RELAY_SECTIONS, SECTION_LENGTH, KEY_VALUE_HEADS * HEAD_WIDTH))


def draw_queries(key, part):
    return drawn_pair(key)[0].astype(jnp.bfloat16)


def draw_key_states(key, part):
    return drawn_pair(key)[1].astype(jnp.bfloat16)


def levels(key, dims, cuts, smallest, high):
    def one(axis_at, blocks):
        heights = jax.random.uniform(jax.random.fold_in(jax.random.fold_in(key, 6), axis_at), (blocks,), jnp.float32, smallest / len(cuts), high / len(cuts))
        return jnp.repeat(jnp.exp(heights), dims[axis_at] // blocks).reshape((-1,) + (1,) * (len(dims) - axis_at - 1))

    gain = one(*cuts[0])
    for cut in cuts[1:]:
        gain = gain * one(*cut)
    return gain


def profile(number_of, total, limit, slope):
    portions = [(1 << 20) // math.isqrt(rank ** slope) + 1 for rank in range(2, number_of + 1)]
    surplus, given = total - limit - (number_of - 1), [1] * (number_of - 1)
    while surplus > 0:
        candidates = [i for i in range(number_of - 1) if given[i] < limit]
        whole, left = sum([portions[i] for i in candidates]), surplus
        for i in candidates:
            addition = min(limit - given[i], max(1, left * portions[i] // whole), surplus)
            given[i] = given[i] + addition
            surplus = surplus - addition
    return np.array([limit] + given)


def uneven_parts(key, number_of, total, most, lean):
    if number_of == 2:
        one = jax.random.randint(key, (), max(1, total - most), min(most, total - 1) + 1)
        return jnp.stack([one, total - one])
    sizes = jnp.asarray(profile(number_of, total, most, lean), jnp.int32)
    couples = (number_of - 1) // 2
    donor, taker = sizes[1:1 + 2 * couples:2], sizes[2:2 + 2 * couples:2]
    slack = jnp.minimum(donor - 1, most - taker)
    moved = jax.random.randint(jax.random.fold_in(key, 1), (couples,), 0, 1 << 20) % (slack + 1)
    sizes = sizes.at[1:1 + 2 * couples:2].set(donor - moved).at[2:2 + 2 * couples:2].set(taker + moved)
    return sizes[jax.random.permutation(jax.random.fold_in(key, 2), number_of)]


def noise(own_key, shape, scale, reach, cuts=(), held_as=jnp.bfloat16):
    level = levels(own_key, shape, cuts, -0.22, 0.18) if cuts else 1.0
    values = jax.random.normal(own_key, shape, jnp.float32) * scale * level
    return jnp.minimum(jnp.maximum(values, -reach), reach).astype(held_as)


def setup_inputs(seed: int = 0) -> dict:
    seeds = jax.random.split(jax.random.key(seed), 7)
    queries = draw_queries(jax.random.fold_in(seeds[6], 71), 0)
    key_states = draw_key_states(jax.random.fold_in(seeds[6], 71), 0)
    section_value_states = noise(seeds[2], (RELAY_SECTIONS, SECTION_LENGTH, KEY_VALUE_HEADS * HEAD_WIDTH), 1.0, 6.0, ((0, 16), (1, 8)))
    out_grad = noise(seeds[3], (RELAY_SECTIONS, SECTION_LENGTH, QUERY_HEADS * HEAD_WIDTH), 0.25, 1.5, ((0, 16), (1, 8)))
    layer_input = noise(seeds[4], (RELAY_SECTIONS, SECTION_LENGTH, D), 1.0, 6.0, ((0, 16), (1, 8)))
    doc_segments = jax.vmap(lambda own: jnp.searchsorted(jnp.cumsum(uneven_parts(own, 4, SECTION_LENGTH, SECTION_LENGTH // 2, 2)), jnp.arange(SECTION_LENGTH), side="right"))(jax.random.split(seeds[5], RELAY_SECTIONS)).reshape((RELAY_SECTIONS, SECTION_LENGTH)).astype(jnp.int32)
    return dict(queries=queries, key_states=key_states, section_value_states=section_value_states, out_grad=out_grad, layer_input=layer_input, doc_segments=doc_segments)


def group_pass(query_group, key_col, value_col, grad_group, allowed):
    scale_factor = 1.0 / math.sqrt(key_col.shape[1])

    def one_head(totals, head_inputs):
        query_one, grad_one = head_inputs
        key_acc, value_acc = totals
        scores = jnp.dot(query_one, key_col.T, preferred_element_type=jnp.float32) * scale_factor
        scores = jnp.where(allowed, scores, -jnp.inf)
        row_max = lax.optimization_barrier(jnp.max(scores, axis=1, keepdims=True))
        weights = jnp.exp(scores - row_max)
        attention = weights / lax.optimization_barrier(jnp.sum(weights, axis=1, keepdims=True))
        probs_low = attention.astype(jnp.bfloat16)
        attended = jnp.dot(probs_low, value_col, preferred_element_type=jnp.float32).astype(jnp.bfloat16)
        attended = lax.optimization_barrier(attended)
        row_delta = lax.optimization_barrier(jnp.sum(grad_one.astype(jnp.float32) * attended.astype(jnp.float32), axis=1, keepdims=True))
        dprobs = jnp.dot(grad_one, value_col.T, preferred_element_type=jnp.float32)
        dscores = (attention * (dprobs - row_delta) * scale_factor).astype(jnp.bfloat16)
        query_part = jnp.dot(dscores, key_col, preferred_element_type=jnp.float32).astype(jnp.bfloat16)
        key_acc = key_acc + jnp.dot(dscores.T, query_one, preferred_element_type=jnp.float32)
        value_acc = value_acc + jnp.dot(probs_low.T, grad_one, preferred_element_type=jnp.float32)
        return ((key_acc, value_acc), query_part)
    starting = jnp.zeros(key_col.shape, jnp.float32)
    (key_acc, value_acc), query_parts = lax.scan(one_head, (starting, starting), (query_group, grad_group))
    return (query_parts, key_acc.astype(jnp.bfloat16), value_acc.astype(jnp.bfloat16))

def attention_grads(query_cols, key_cols, value_cols, grad_cols, doc_ids):
    length = query_cols.shape[0]
    kv_heads = key_cols.shape[1] // HEAD_WIDTH
    q_heads = query_cols.shape[1] // HEAD_WIDTH
    group_size = q_heads // kv_heads
    position = jnp.arange(length, dtype=jnp.int32)
    allowed = (position[:, None] >= position[None, :]) & (doc_ids[:, None] == doc_ids[None, :])
    query_split = query_cols.reshape(length, kv_heads, group_size, HEAD_WIDTH).transpose(1, 2, 0, 3)
    grad_split = grad_cols.reshape(length, kv_heads, group_size, HEAD_WIDTH).transpose(1, 2, 0, 3)
    key_split = key_cols.reshape(length, kv_heads, HEAD_WIDTH).transpose(1, 0, 2)
    value_split = value_cols.reshape(length, kv_heads, HEAD_WIDTH).transpose(1, 0, 2)

    def per_group(inputs):
        return group_pass(inputs[0], inputs[1], inputs[2], inputs[3], allowed)
    query_parts, key_parts, value_parts = lax.map(per_group, (query_split, key_split, value_split, grad_split))
    query_out = query_parts.transpose(2, 0, 1, 3).reshape(length, q_heads * HEAD_WIDTH)
    key_out = key_parts.transpose(1, 0, 2).reshape(length, kv_heads * HEAD_WIDTH)
    value_out = value_parts.transpose(1, 0, 2).reshape(length, kv_heads * HEAD_WIDTH)
    return (query_out, key_out, value_out)

def reference(queries, key_states, section_value_states, out_grad, layer_input, doc_segments):

    def per_section(inputs):
        query_cols, key_cols, value_cols, grad_cols, layer_rows, doc_ids = inputs
        query_out, key_out, value_out = attention_grads(query_cols, key_cols, value_cols, grad_cols, doc_ids)
        section_grad = jnp.dot(layer_rows.T, value_out, preferred_element_type=jnp.float32)
        return (query_out, key_out, section_grad)
    query_grad, key_grad, section_grad = lax.map(per_section, (queries, key_states, section_value_states, out_grad, layer_input, doc_segments))
    weight_grad = (section_grad + section_grad[::-1]).astype(jnp.bfloat16)
    return (query_grad, key_grad, weight_grad)
```

```python
import math

import jax
import jax.numpy as jnp
from jax import lax
from jax.experimental import pallas as pl
from jax.experimental.pallas import tpu as pltpu
from jax.sharding import PartitionSpec as P

MESH = pl.DeviceIdType.MESH
W = 128
G = 8
REP = 8
NSLOT = 5
NB = 4
GB = G // NB
ROWS = 512
SCALE = 1.0 / math.sqrt(W)
LOG2E = 1.4426950408889634
BF = jnp.bfloat16
F32 = jnp.float32


def dot(a, b, ca, cb):
    return lax.dot_general(a, b, (((ca,), (cb,)), ((), ())), preferred_element_type=F32)


def kernel(
    q_hbm, k_ref, v_ref, do_hbm, l_hbm, doc_ref,
    dq_hbm, dk_hbm, wg_hbm,
    q_vm, do_vm, kvx, docx, bias, tx, rx, own, dvall, lall, wout, dq_vm, dk_vm, pl_vm, ds_vm,
    in_sem, kv_ss, kv_rs, doc_ss, doc_rs, l_ss, l_rs, p_ss, p_rs, x1_ss, x1_rs, x2_ss, x2_rs,
    o_ss, o_rs, out_sem,
):
    s = lax.axis_index("section")
    j = lax.axis_index("seq")
    sec = s // 8
    s0 = s + sec * (15 - 2 * s)
    me = sec * 8 + j
    y = j // 2
    xh = j % 2

    def dev(sec2, j2):
        return (s0 + sec2 * (15 - 2 * s0), j2)

    def remote(src, dst, ss, rs, to):
        return pltpu.make_async_remote_copy(
            src_ref=src, dst_ref=dst, send_sem=ss, recv_sem=rs, device_id=to, device_id_type=MESH
        )

    q_in = pltpu.make_async_copy(q_hbm, q_vm, in_sem.at[0])
    do_in = pltpu.make_async_copy(do_hbm, do_vm, in_sem.at[1])
    q_in.start()
    do_in.start()
    l_own = pltpu.make_async_copy(
        l_hbm.at[:, pl.ds(pl.multiple_of(me * ROWS, ROWS), ROWS)], lall.at[sec, j], in_sem.at[2]
    )
    l_own.start()

    barrier = pltpu.get_barrier_semaphore()

    def greet(k, c):
        r = (me + k) % 16
        pl.semaphore_signal(barrier, inc=1, device_id=dev(r // 8, r % 8), device_id_type=MESH)
        return c

    lax.fori_loop(1, 16, greet, 0)

    for g in range(G):
        kvx[g, 0, 0] = k_ref[:, g * W:(g + 1) * W]
        kvx[g, 1, 0] = v_ref[:, g * W:(g + 1) * W]
    docx[0] = jnp.broadcast_to(doc_ref[...], (8, W))
    for d in range(1, NSLOT):
        @pl.when(j < d)
        def _():
            kvx[:, :, d] = jnp.zeros((G, 2, W, W), BF)
            docx[d] = jnp.zeros((8, W), jnp.int32)

    pl.semaphore_wait(barrier, 15)

    def kv_copy(b, d):
        hs = pl.ds(b * GB, GB)
        return remote(
            kvx.at[hs, :, 0], kvx.at[hs, :, d], kv_ss.at[b, d], kv_rs.at[b, d], (s, j + d)
        )

    def doc_copy(d):
        return remote(docx.at[0], docx.at[d], doc_ss.at[d], doc_rs.at[d], (s, j + d))

    for d in range(1, NSLOT):
        @pl.when(j + d < 8)
        def _():
            doc_copy(d).start()

    def send_kv(b, c):
        for d in range(1, NSLOT):
            @pl.when(j + d < 8)
            def _():
                kv_copy(b, d).start()
        return c

    lax.fori_loop(0, NB, send_kv, 0)

    def l_copy(k):
        r = (me + k) % 16
        return remote(
            l_hbm.at[:, pl.ds(pl.multiple_of(r * ROWS, ROWS), ROWS)], lall.at[sec, j],
            l_ss.at[k], l_rs.at[k], dev(r // 8, r % 8),
        )

    def send_l(k, c):
        l_copy(k).start()
        return c

    lax.fori_loop(1, 16, send_l, 0)

    for d in range(1, NSLOT):
        @pl.when(j >= d)
        def _():
            doc_copy(d).wait_recv()

    row = lax.broadcasted_iota(jnp.int32, (W, W), 0)
    col = lax.broadcasted_iota(jnp.int32, (W, W), 1)
    q_doc = jnp.broadcast_to(docx[0, 0:1], (W, W)).astype(F32)
    for d in range(NSLOT):
        key_doc = jnp.broadcast_to(docx[d, 0:1], (W, W)).astype(F32).T
        seen = (key_doc == q_doc) & (j >= d)
        if d == 0:
            seen = seen & (row <= col)
        bias[d * W:(d + 1) * W] = jnp.where(seen, 0.0, -jnp.inf).astype(F32)

    q_in.wait()
    do_in.wait()

    def attention(b, g):
        keys = kvx.at[g, 0]
        values = kvx.at[g, 1]

        def pair(p, c):
            at = pl.multiple_of((g * REP + 2 * p) * W, 2 * W)
            q2 = q_vm[:, pl.ds(at, 2 * W)]
            o2 = do_vm[:, pl.ds(at, 2 * W)]
            q2 = jnp.concatenate([q2[:, :W], q2[:, W:]], axis=0)
            o2 = jnp.concatenate([o2[:, :W], o2[:, W:]], axis=0)
            t = []
            m = None
            for d in range(NSLOT):
                bd = bias[d * W:(d + 1) * W]
                td = dot(keys[d], q2, 1, 1) * (SCALE * LOG2E) + jnp.concatenate([bd, bd], axis=1)
                t.append(td)
                md = jnp.max(td, axis=0, keepdims=True)
                m = md if m is None else jnp.maximum(m, md)
            total = None
            for d in range(NSLOT):
                t[d] = jnp.exp2(t[d] - m)
                ld = jnp.sum(t[d], axis=0, keepdims=True)
                total = ld if total is None else total + ld
            inv = 1.0 / total
            delta = None
            dps = []
            out = pl.ds(pl.multiple_of(p * 2 * W, 2 * W), 2 * W)
            for d in range(NSLOT):
                low = (t[d] * inv).astype(BF)
                pl_vm[d * W:(d + 1) * W, out] = low
                dp = dot(values[d], o2, 1, 1)
                dps.append(dp)
                dd = jnp.sum(low.astype(F32) * dp, axis=0, keepdims=True)
                delta = dd if delta is None else delta + dd
            inv = inv * SCALE
            for d in range(NSLOT):
                ds_vm[d * W:(d + 1) * W, out] = (t[d] * inv * (dps[d] - delta)).astype(BF)
            return c

        lax.fori_loop(0, REP // 2, pair, 0)

        k_all = keys[...].reshape(NSLOT * W, W)
        k_t = k_all.T
        qs = jnp.concatenate(
            [q_vm[:, pl.ds(pl.multiple_of((g * REP + h) * W, W), W)] for h in range(REP)], axis=0
        )
        dos = jnp.concatenate(
            [do_vm[:, pl.ds(pl.multiple_of((g * REP + h) * W, W), W)] for h in range(REP)], axis=0
        )
        for d in range(NSLOT):
            dk = dot(ds_vm[d * W:(d + 1) * W], qs, 1, 0)
            dv = dot(pl_vm[d * W:(d + 1) * W], dos, 1, 0)
            if d == 0:
                own[g, 0] = dk
                own[g, 1] = dv
            else:
                tx[g, 0, d - 1] = dk.astype(BF)
                tx[g, 1, d - 1] = dv.astype(BF)
        for h in range(REP):
            dqt = dot(k_t, ds_vm[:, h * W:(h + 1) * W], 1, 0)
            dq_vm[:, pl.ds(pl.multiple_of((g * REP + h) * W, W), W)] = dqt.T.astype(BF)

    def part_copy(b, d):
        hs = pl.ds(b * GB, GB)
        return remote(
            tx.at[hs, :, d - 1], rx.at[hs, :, d - 1], p_ss.at[b, d], p_rs.at[b, d], (s, j - d)
        )

    def x_peer(e):
        return (sec + e % 2) % 2, (xh + e // 2) % 2

    def gather_one(b, e, along_x):
        mine = dvall.at[b, sec, y, xh]
        if along_x:
            sec2, xh2 = x_peer(e)
            to = dev(sec2, 2 * y + xh2)
        else:
            to = dev(sec, 2 * ((y + e) % 4) + xh)
        return remote(mine, mine, x1_ss.at[b, e], x1_rs.at[b, e], to)

    def gather_two(b, e, along_x):
        if along_x:
            held = dvall.at[b, :, y]
            to = dev(sec, 2 * ((y + e) % 4) + xh)
        else:
            held = dvall.at[b, sec, :, xh]
            sec2, xh2 = x_peer(e)
            to = dev(sec2, 2 * y + xh2)
        return remote(held, held, x2_ss.at[b, e], x2_rs.at[b, e], to)

    def both(b, act):
        @pl.when(b % 2 == 0)
        def _():
            act(True)

        @pl.when(b % 2 == 1)
        def _():
            act(False)

    def reduce(b):
        for d in range(1, NSLOT):
            @pl.when(j + d < 8)
            def _():
                part_copy(b, d).wait_recv()
                for gg in range(GB):
                    g = b * GB + gg
                    own[g] = own[g] + rx[g, :, d - 1].astype(F32)
        for gg in range(GB):
            g = b * GB + gg
            dk_vm[:, pl.ds(pl.multiple_of(g * W, W), W)] = own[g, 0].astype(BF)
            dvall[b, sec, y, xh, :, gg * W:(gg + 1) * W] = own[g, 1].astype(BF)

        def act(along_x):
            for e in range(1, 4):
                gather_one(b, e, along_x).start()

        both(b, act)

    def forward(b):
        def act(along_x):
            for e in range(1, 4):
                gather_one(b, e, along_x).wait_recv()
            for e in range(1, 4):
                gather_two(b, e, along_x).start()

        both(b, act)

    def out_copies(b, act):
        for hh in range(GB):
            for sec2 in range(2):
                target = sec2 * 8 + b * GB + hh
                src = wout.at[b, hh]
                dst = wg_hbm.at[pl.ds(pl.multiple_of(me * ROWS, ROWS), ROWS)]

                @pl.when(target != me)
                def _():
                    act(remote(
                        src, dst, o_ss.at[b, hh * 2 + sec2], o_rs.at[me], dev(sec2, b * GB + hh)
                    ), None)

                @pl.when(target == me)
                def _():
                    act(None, pltpu.make_async_copy(src, dst, out_sem.at[2]))

    def start_out(far, near):
        (far if near is None else near).start()

    def end_out(far, near):
        if near is None:
            far.wait_send()
        else:
            near.wait()

    def weights(b):
        def act(along_x):
            for e in range(1, 4):
                gather_two(b, e, along_x).wait_recv()

        both(b, act)

        @pl.when(b == 0)
        def _():
            l_own.wait()

            def wait_l(k, c):
                l_copy(k).wait_recv()
                return c

            lax.fori_loop(1, 16, wait_l, 0)

        dv = dvall[b].reshape(16 * W, GB * W)
        la = lall[...].reshape(16 * W, ROWS)
        res = dot(la, dv, 0, 0)
        for hh in range(GB):
            wout[b, hh] = res[:, hh * W:(hh + 1) * W].astype(BF)
        out_copies(b, start_out)

    def step(i, c):
        @pl.when(i < NB)
        def _():
            for d in range(1, NSLOT):
                @pl.when(j >= d)
                def _():
                    kv_copy(i, d).wait_recv()

            def group(gg, c2):
                attention(i, i * GB + gg)
                return c2

            lax.fori_loop(0, GB, group, 0)
            for d in range(1, NSLOT):
                @pl.when(j >= d)
                def _():
                    part_copy(i, d).start()

        @pl.when((i >= 1) & (i < NB + 1))
        def _():
            reduce(i - 1)

        @pl.when((i >= 2) & (i < NB + 2))
        def _():
            forward(i - 2)

        @pl.when(i >= 3)
        def _():
            weights(i - 3)

        return c

    lax.fori_loop(0, NB + 3, step, 0)

    dq_out = pltpu.make_async_copy(dq_vm, dq_hbm, out_sem.at[0])
    dk_out = pltpu.make_async_copy(dk_vm, dk_hbm, out_sem.at[1])
    dq_out.start()
    dk_out.start()

    def end_batch(b, c):
        for d in range(1, NSLOT):
            @pl.when(j + d < 8)
            def _():
                kv_copy(b, d).wait_send()

            @pl.when(j >= d)
            def _():
                part_copy(b, d).wait_send()

        def act(along_x):
            for e in range(1, 4):
                gather_one(b, e, along_x).wait_send()
                gather_two(b, e, along_x).wait_send()

        both(b, act)
        out_copies(b, end_out)
        return c

    lax.fori_loop(0, NB, end_batch, 0)
    for d in range(1, NSLOT):
        @pl.when(j + d < 8)
        def _():
            doc_copy(d).wait_send()

    def end_l(k, c):
        l_copy(k).wait_send()
        r = (me + k) % 16
        remote(
            wout.at[0, 0], wg_hbm.at[pl.ds(pl.multiple_of(r * ROWS, ROWS), ROWS)],
            o_ss.at[0, 0], o_rs.at[r], dev(r // 8, r % 8),
        ).wait_recv()
        return c

    lax.fori_loop(1, 16, end_l, 0)
    dq_out.wait()
    dk_out.wait()


def local(queries, key_states, section_value_states, out_grad, layer_input, doc_segments):
    hbm = pl.BlockSpec(memory_space=pl.ANY)
    vmem = pl.BlockSpec(memory_space=pltpu.VMEM)
    dma = pltpu.SemaphoreType.DMA
    dq, dk, wg = pl.pallas_call(
        kernel,
        out_shape=(
            jax.ShapeDtypeStruct((W, 8192), BF),
            jax.ShapeDtypeStruct((W, G * W), BF),
            jax.ShapeDtypeStruct((8192, W), BF),
        ),
        in_specs=[hbm, vmem, vmem, hbm, hbm, vmem],
        out_specs=(hbm, hbm, hbm),
        scratch_shapes=[
            pltpu.VMEM((W, 8192), BF),
            pltpu.VMEM((W, 8192), BF),
            pltpu.VMEM((G, 2, NSLOT, W, W), BF),
            pltpu.VMEM((NSLOT, 8, W), jnp.int32),
            pltpu.VMEM((NSLOT * W, W), F32),
            pltpu.VMEM((G, 2, NSLOT - 1, W, W), BF),
            pltpu.VMEM((G, 2, NSLOT - 1, W, W), BF),
            pltpu.VMEM((G, 2, W, W), F32),
            pltpu.VMEM((NB, 2, 4, 2, W, GB * W), BF),
            pltpu.VMEM((2, 8, W, ROWS), BF),
            pltpu.VMEM((NB, GB, ROWS, W), BF),
            pltpu.VMEM((W, 8192), BF),
            pltpu.VMEM((W, G * W), BF),
            pltpu.VMEM((NSLOT * W, REP * W), BF),
            pltpu.VMEM((NSLOT * W, REP * W), BF),
            dma((3,)),
            dma((NB, NSLOT)), dma((NB, NSLOT)),
            dma((NSLOT,)), dma((NSLOT,)),
            dma((16,)), dma((16,)),
            dma((NB, NSLOT)), dma((NB, NSLOT)),
            dma((NB, 4)), dma((NB, 4)),
            dma((NB, 4)), dma((NB, 4)),
            dma((NB, 4)), dma((16,)),
            dma((3,)),
        ],
        compiler_params=pltpu.CompilerParams(
            collective_id=0, has_side_effects=True, vmem_limit_bytes=56 << 20
        ),
        cost_estimate=pl.CostEstimate(
            flops=10_000_000_000, bytes_accessed=12_000_000, transcendentals=5_000_000
        ),
        name="attention_weight_grad",
    )(
        queries[0], key_states[0], section_value_states[0], out_grad[0], layer_input[0],
        doc_segments,
    )
    return dq[None], dk[None], wg[None]


def solution(mesh):
    rows = P("section", "seq", None)
    return jax.shard_map(
        local,
        mesh=mesh,
        in_specs=(rows, rows, rows, rows, rows, P("section", "seq")),
        out_specs=(rows, rows, P("section", None, "seq")),
        check_vma=False,
    )
```

```python
import math

import jax
import jax.numpy as jnp
from jax import lax
from jax.experimental import pallas as pl
from jax.experimental.pallas import tpu as pltpu
from jax.sharding import PartitionSpec as P

MESH = pl.DeviceIdType.MESH
W = 128
G = 8
REP = 8
NSLOT = 5
NB = 4
GB = G // NB
ROWS = 1024
SCALE = 1.0 / math.sqrt(W)
LOG2E = 1.4426950408889634
BF = jnp.bfloat16
F32 = jnp.float32


def dot(a, b, ca, cb):
    return lax.dot_general(a, b, (((ca,), (cb,)), ((), ())), preferred_element_type=F32)


def kernel(
    q_hbm, k_ref, v_ref, do_hbm, l_hbm, doc_ref,
    dq_hbm, dk_hbm, wg_hbm,
    q_vm, do_vm, kv, docx, bias, prob, low_vm, ds_vm, acc, xtx, xrx, ytx, yrx, dvall, lall, lt,
    keep, wtx, wrx, wout, dq_vm, dk_vm,
    in_sem, doc_ss, doc_rs, ky_ss, ky_rs, kx_ss, kx_rs, l_ss, l_rs, px_ss, px_rs, py_ss, py_rs,
    gx_ss, gx_rs, gy_ss, gy_rs, w_ss, w_rs, o_ss, o_rs, out_sem,
):
    s = lax.axis_index("section")
    j = lax.axis_index("seq")
    sec = s // 8
    y = j // 2
    xh = j % 2
    mine = ((sec + xh) % 2) * 4 + y
    partner = j + 1 - 2 * xh

    def remote(src, dst, ss, rs, to):
        return pltpu.make_async_remote_copy(
            src_ref=src, dst_ref=dst, send_sem=ss, recv_sem=rs, device_id=to, device_id_type=MESH
        )

    def of_section(sec2):
        return s + (sec2 + sec - 2 * sec * sec2) * (15 - 2 * s)

    def holder(r):
        return of_section((r // 4 + xh) % 2), 2 * (r % 4) + xh

    def rows_of(r):
        return pl.ds(pl.multiple_of(r * ROWS, ROWS), ROWS)

    def heads(b):
        return pl.ds(b * GB, GB)

    q_in = pltpu.make_async_copy(q_hbm, q_vm, in_sem.at[0])
    do_in = pltpu.make_async_copy(do_hbm, do_vm, in_sem.at[1])
    l_own = pltpu.make_async_copy(l_hbm.at[:, rows_of(mine)], lall.at[sec, y], in_sem.at[2])
    q_in.start()
    do_in.start()
    l_own.start()

    barrier = pltpu.get_barrier_semaphore()

    def greet(to):
        pl.semaphore_signal(barrier, inc=1, device_id=to, device_id_type=MESH)

    def greet_own(k, c):
        greet((s, (j + k) % 8))
        return c

    def greet_mirror(k, c):
        greet((15 - s, 2 * k + xh))
        return c

    lax.fori_loop(1, 8, greet_own, 0)
    lax.fori_loop(0, 4, greet_mirror, 0)
    greet((15 - s, partner))

    for g in range(G):
        kv[0, g, 0] = k_ref[:, g * W:(g + 1) * W]
        kv[1, g, 0] = v_ref[:, g * W:(g + 1) * W]
    docx[0] = jnp.broadcast_to(doc_ref[...], (8, W))
    for d in range(1, NSLOT):
        @pl.when(j < d)
        def _():
            kv[:, :, d] = jnp.zeros((2, G, W, W), BF)
            docx[d] = jnp.zeros((8, W), jnp.int32)

    pl.semaphore_wait(barrier, 12)

    def doc_copy(d):
        return remote(docx.at[0], docx.at[d], doc_ss.at[d], doc_rs.at[d], (s, j + d))

    def kv_y(kind, b, n):
        return remote(
            kv.at[kind, heads(b), 0], kv.at[kind, heads(b), 2 * n + 2],
            ky_ss.at[kind, b, n], ky_rs.at[kind, b, n], (s, j + 2 * n + 2),
        )

    def kv_x(kind, b, n):
        return remote(
            kv.at[kind, heads(b), 2 * n + 2 * xh], kv.at[kind, heads(b), 2 * n + 1],
            kx_ss.at[kind, b, n], kx_rs.at[kind, b, n], (s, partner),
        )

    def send_kv(kind, b):
        @pl.when(xh == 0)
        def _():
            kv_x(kind, b, 0).start()

        for n in range(2):
            @pl.when(j + 2 * n + 2 < 8)
            def _():
                kv_y(kind, b, n).start()

    def relay_kv(kind, b):
        for n in range(2):
            @pl.when(j >= 2 * n + 2)
            def _():
                kv_y(kind, b, n).wait_recv()

        for n in range(2):
            @pl.when((j >= 2 * n + 2 * xh) & (n + xh > 0))
            def _():
                kv_x(kind, b, n).start()

    def got_kv(kind, b):
        for n in range(2):
            @pl.when(j >= 2 * n + 1)
            def _():
                kv_x(kind, b, n).wait_recv()

    for d in range(1, NSLOT):
        @pl.when(j + d < 8)
        def _():
            doc_copy(d).start()

    def send_all(b, c):
        send_kv(0, b)
        return c

    lax.fori_loop(0, NB, send_all, 0)

    def send_v(b, c):
        send_kv(1, b)
        return c

    lax.fori_loop(0, NB, send_v, 0)

    def l_copy(k):
        r = (mine + k) % 8
        return remote(l_hbm.at[:, rows_of(r)], lall.at[sec, y], l_ss.at[k], l_rs.at[k], holder(r))

    def send_l(k, c):
        l_copy(k).start()
        return c

    lax.fori_loop(1, 8, send_l, 0)

    for d in range(1, NSLOT):
        @pl.when(j >= d)
        def _():
            doc_copy(d).wait_recv()

    row = lax.broadcasted_iota(jnp.int32, (W, W), 0)
    col = lax.broadcasted_iota(jnp.int32, (W, W), 1)
    q_doc = jnp.broadcast_to(docx[0, 0:1], (W, W)).astype(F32)
    for d in range(NSLOT):
        key_doc = jnp.broadcast_to(docx[d, 0:1], (W, W)).astype(F32).T
        seen = (key_doc == q_doc) & (j >= d)
        if d == 0:
            seen = seen & (row <= col)
        bias[d * W:(d + 1) * W] = jnp.where(seen, 0.0, -jnp.inf).astype(F32)

    q_in.wait()
    do_in.wait()

    def two_heads(ref, g, p):
        both = ref[:, pl.ds(pl.multiple_of((g * REP + 2 * p) * W, 2 * W), 2 * W)]
        return jnp.concatenate([both[:, :W], both[:, W:]], axis=0)

    def group_rows(ref, g):
        return jnp.concatenate(
            [ref[:, pl.ds(pl.multiple_of((g * REP + h) * W, W), W)] for h in range(REP)], axis=0
        )

    def part_sums(kind, g, left, right):
        for d in range(NSLOT):
            part = dot(left[d * W:(d + 1) * W], right, 1, 0)
            if d % 2 == 0:
                acc[kind, g, d // 2] = part
            else:
                xtx[kind, g, d // 2] = part.astype(BF)

    def probabilities(g):
        keys = kv.at[0, g]

        def pair(p, c):
            q2 = two_heads(q_vm, g, p)
            t = []
            m = None
            for d in range(NSLOT):
                bd = bias[d * W:(d + 1) * W]
                td = dot(keys[d], q2, 1, 1) * (SCALE * LOG2E) + jnp.concatenate([bd, bd], axis=1)
                t.append(td)
                md = jnp.max(td, axis=0, keepdims=True)
                m = md if m is None else jnp.maximum(m, md)
            total = None
            for d in range(NSLOT):
                t[d] = jnp.exp2(t[d] - m)
                ld = jnp.sum(t[d], axis=0, keepdims=True)
                total = ld if total is None else total + ld
            inv = 1.0 / total
            out = pl.ds(pl.multiple_of(p * 2 * W, 2 * W), 2 * W)
            for d in range(NSLOT):
                pd = t[d] * inv
                prob[g, p, d * W:(d + 1) * W] = pd
                low_vm[d * W:(d + 1) * W, out] = pd.astype(BF)
            return c

        lax.fori_loop(0, REP // 2, pair, 0)
        part_sums(1, g, low_vm, group_rows(do_vm, g))

    def score_grads(g):
        values = kv.at[1, g]

        def pair(p, c):
            o2 = two_heads(do_vm, g, p)
            delta = None
            dps = []
            for d in range(NSLOT):
                dp = dot(values[d], o2, 1, 1)
                dps.append(dp)
                low = prob[g, p, d * W:(d + 1) * W].astype(BF).astype(F32)
                dd = jnp.sum(low * dp, axis=0, keepdims=True)
                delta = dd if delta is None else delta + dd
            out = pl.ds(pl.multiple_of(p * 2 * W, 2 * W), 2 * W)
            for d in range(NSLOT):
                pd = prob[g, p, d * W:(d + 1) * W]
                ds_vm[d * W:(d + 1) * W, out] = (pd * ((dps[d] - delta) * SCALE)).astype(BF)
            return c

        lax.fori_loop(0, REP // 2, pair, 0)
        part_sums(0, g, ds_vm, group_rows(q_vm, g))
        k_t = kv[0, g].reshape(NSLOT * W, W).T
        for h in range(REP):
            dqt = dot(k_t, ds_vm[:, h * W:(h + 1) * W], 1, 0)
            dq_vm[:, pl.ds(pl.multiple_of((g * REP + h) * W, W), W)] = dqt.T.astype(BF)

    def part_x(kind, b, n):
        return remote(
            xtx.at[kind, heads(b), n], xrx.at[kind, heads(b), n],
            px_ss.at[kind, b, n], px_rs.at[kind, b, n], (s, partner),
        )

    def part_y(kind, b, n):
        return remote(
            ytx.at[kind, heads(b), n], yrx.at[kind, heads(b), n],
            py_ss.at[kind, b, n], py_rs.at[kind, b, n], (s, j - 2 * n - 2),
        )

    def send_parts(kind, b):
        for n in range(2):
            @pl.when(j >= 2 * n + 1)
            def _():
                part_x(kind, b, n).start()

    def cross_parts(kind, b):
        for n in range(2):
            @pl.when(partner >= 2 * n + 1)
            def _():
                part_x(kind, b, n).wait_recv()
                for gg in range(GB):
                    g = b * GB + gg
                    acc[kind, g, n + xh] = acc[kind, g, n + xh] + xrx[kind, g, n].astype(F32)

        for n in range(2):
            @pl.when(j >= 2 * n + 2)
            def _():
                ytx[kind, heads(b), n] = acc[kind, heads(b), n + 1].astype(BF)
                part_y(kind, b, n).start()

    def own_sums(kind, b):
        for n in range(2):
            @pl.when(j + 2 * n + 2 < 8)
            def _():
                part_y(kind, b, n).wait_recv()
                for gg in range(GB):
                    g = b * GB + gg
                    acc[kind, g, 0] = acc[kind, g, 0] + yrx[kind, g, n].astype(F32)

    def gather_x(b):
        block = dvall.at[b, sec, y]
        return remote(block, block, gx_ss.at[b], gx_rs.at[b], (15 - s, j))

    def gather_y(b, e):
        blocks = dvall.at[b, :, y]
        to = (s, 2 * ((y + e) % 4) + xh)
        return remote(blocks, blocks, gy_ss.at[b, e], gy_rs.at[b, e], to)

    def value_grads(b):
        own_sums(1, b)
        for gg in range(GB):
            dvall[b, sec, y, :, gg * W:(gg + 1) * W] = acc[1, b * GB + gg, 0].astype(BF)
        gather_x(b).start()

    def key_grads(b):
        own_sums(0, b)
        for gg in range(GB):
            g = b * GB + gg
            dk_vm[:, pl.ds(pl.multiple_of(g * W, W), W)] = acc[0, g, 0].astype(BF)

    def forward(b):
        gather_x(b).wait_recv()
        for e in range(1, 4):
            gather_y(b, e).start()

    def w_copy(b):
        return remote(wtx.at[b], wrx.at[b], w_ss.at[b], w_rs.at[b], (15 - s, partner))

    def weights(b):
        for e in range(1, 4):
            gather_y(b, e).wait_recv()

        @pl.when(b == 0)
        def _():
            l_own.wait()

            def wait_l(k, c):
                l_copy(k).wait_recv()
                return c

            lax.fori_loop(1, 8, wait_l, 0)
            for r in range(ROWS // W):
                la = lall[:, :, :, r * W:(r + 1) * W].reshape(8 * W, W)
                lt[r * W:(r + 1) * W] = la.T

        dv = dvall[b].reshape(8 * W, GB * W)

        def chunk(r, c):
            at = pl.ds(pl.multiple_of(r * 2 * W, 2 * W), 2 * W)
            res = dot(lt[at], dv, 1, 0)
            keep[b, at] = jnp.where(xh == 0, res[:, :W], res[:, W:])
            wtx[b, at] = jnp.where(xh == 0, res[:, W:], res[:, :W]).astype(BF)
            return c

        lax.fori_loop(0, ROWS // (2 * W), chunk, 0)
        w_copy(b).start()

    def out_copies(b, far, near):
        for sec2 in range(2):
            at_home = (sec2 == sec) & (b == y)
            src, dst = wout.at[b], wg_hbm.at[rows_of(mine)]

            @pl.when(jnp.logical_not(at_home))
            def _():
                far(remote(
                    src, dst, o_ss.at[b, sec2], o_rs.at[mine], (of_section(sec2), 2 * b + xh)
                ))

            @pl.when(at_home)
            def _():
                near(pltpu.make_async_copy(src, dst, out_sem.at[2]))

    def finish(b):
        w_copy(b).wait_recv()
        wout[b] = (keep[b] + wrx[b].astype(F32)).astype(BF)
        out_copies(b, lambda c: c.start(), lambda c: c.start())

    relay_kv(0, 0)

    def step(i, c):
        def at(first, do, *args):
            @pl.when((i >= first) & (i < first + NB))
            def _():
                do(*args, i - first)

        @pl.when(i < NB - 1)
        def _():
            relay_kv(0, i + 1)

        @pl.when((i >= NB - 1) & (i < 2 * NB - 1))
        def _():
            relay_kv(1, i - (NB - 1))

        def first_half(b):
            got_kv(0, b)

            def group(gg, c2):
                probabilities(b * GB + gg)
                return c2

            lax.fori_loop(0, GB, group, 0)
            send_parts(1, b)

        def second_half(b):
            got_kv(1, b)

            def group(gg, c2):
                score_grads(b * GB + gg)
                return c2

            lax.fori_loop(0, GB, group, 0)
            send_parts(0, b)

        at(0, first_half)
        at(1, cross_parts, 1)
        at(2, value_grads)
        at(3, forward)
        at(4, weights)
        at(5, finish)
        at(NB, second_half)
        at(NB + 1, cross_parts, 0)
        at(NB + 2, key_grads)
        return c

    lax.fori_loop(0, 2 * NB + 2, step, 0)

    dq_out = pltpu.make_async_copy(dq_vm, dq_hbm, out_sem.at[0])
    dk_out = pltpu.make_async_copy(dk_vm, dk_hbm, out_sem.at[1])
    dq_out.start()
    dk_out.start()

    def end_batch(b, c):
        for kind in range(2):
            @pl.when(xh == 0)
            def _():
                kv_x(kind, b, 0).wait_send()

            for n in range(2):
                @pl.when(j + 2 * n + 2 < 8)
                def _():
                    kv_y(kind, b, n).wait_send()

                @pl.when((j >= 2 * n + 2 * xh) & (n + xh > 0))
                def _():
                    kv_x(kind, b, n).wait_send()

                @pl.when(j >= 2 * n + 1)
                def _():
                    part_x(kind, b, n).wait_send()

                @pl.when(j >= 2 * n + 2)
                def _():
                    part_y(kind, b, n).wait_send()

        gather_x(b).wait_send()
        for e in range(1, 4):
            gather_y(b, e).wait_send()
        w_copy(b).wait_send()
        out_copies(b, lambda c: c.wait_send(), lambda c: c.wait())
        return c

    lax.fori_loop(0, NB, end_batch, 0)
    for d in range(1, NSLOT):
        @pl.when(j + d < 8)
        def _():
            doc_copy(d).wait_send()

    def end_l(k, c):
        l_copy(k).wait_send()
        r = (mine + k) % 8
        remote(
            wout.at[0], wg_hbm.at[rows_of(r)], o_ss.at[0, 0], o_rs.at[r], holder(r)
        ).wait_recv()
        return c

    lax.fori_loop(1, 8, end_l, 0)
    dq_out.wait()
    dk_out.wait()


def local(queries, key_states, section_value_states, out_grad, layer_input, doc_segments):
    hbm = pl.BlockSpec(memory_space=pl.ANY)
    vmem = pl.BlockSpec(memory_space=pltpu.VMEM)
    dma = pltpu.SemaphoreType.DMA
    dq, dk, wg = pl.pallas_call(
        kernel,
        out_shape=(
            jax.ShapeDtypeStruct((W, 8192), BF),
            jax.ShapeDtypeStruct((W, G * W), BF),
            jax.ShapeDtypeStruct((8192, W), BF),
        ),
        in_specs=[hbm, vmem, vmem, hbm, hbm, vmem],
        out_specs=(hbm, hbm, hbm),
        scratch_shapes=[
            pltpu.VMEM((W, 8192), BF),
            pltpu.VMEM((W, 8192), BF),
            pltpu.VMEM((2, G, NSLOT, W, W), BF),
            pltpu.VMEM((NSLOT, 8, W), jnp.int32),
            pltpu.VMEM((NSLOT * W, W), F32),
            pltpu.VMEM((G, REP // 2, NSLOT * W, 2 * W), F32),
            pltpu.VMEM((NSLOT * W, REP * W), BF),
            pltpu.VMEM((NSLOT * W, REP * W), BF),
            pltpu.VMEM((2, G, 3, W, W), F32),
            pltpu.VMEM((2, G, 2, W, W), BF),
            pltpu.VMEM((2, G, 2, W, W), BF),
            pltpu.VMEM((2, G, 2, W, W), BF),
            pltpu.VMEM((2, G, 2, W, W), BF),
            pltpu.VMEM((NB, 2, 4, W, GB * W), BF),
            pltpu.VMEM((2, 4, W, ROWS), BF),
            pltpu.VMEM((ROWS, 8 * W), BF),
            pltpu.VMEM((NB, ROWS, W), F32),
            pltpu.VMEM((NB, ROWS, W), BF),
            pltpu.VMEM((NB, ROWS, W), BF),
            pltpu.VMEM((NB, ROWS, W), BF),
            pltpu.VMEM((W, 8192), BF),
            pltpu.VMEM((W, G * W), BF),
            dma((3,)),
            dma((NSLOT,)), dma((NSLOT,)),
            dma((2, NB, 2)), dma((2, NB, 2)),
            dma((2, NB, 2)), dma((2, NB, 2)),
            dma((8,)), dma((8,)),
            dma((2, NB, 2)), dma((2, NB, 2)),
            dma((2, NB, 2)), dma((2, NB, 2)),
            dma((NB,)), dma((NB,)),
            dma((NB, 4)), dma((NB, 4)),
            dma((NB,)), dma((NB,)),
            dma((NB, 2)), dma((8,)),
            dma((3,)),
        ],
        compiler_params=pltpu.CompilerParams(
            collective_id=0, has_side_effects=True, vmem_limit_bytes=58 << 20
        ),
        cost_estimate=pl.CostEstimate(
            flops=10_000_000_000, bytes_accessed=12_000_000, transcendentals=5_000_000
        ),
        name="attention_weight_grad",
    )(
        queries[0], key_states[0], section_value_states[0], out_grad[0], layer_input[0],
        doc_segments,
    )
    return dq[None], dk[None], wg[None]


def solution(mesh):
    rows = P("section", "seq", None)
    return jax.shard_map(
        local,
        mesh=mesh,
        in_specs=(rows, rows, rows, rows, rows, P("section", "seq")),
        out_specs=(rows, rows, P("section", None, "seq")),
        check_vma=False,
    )
```

```python
import math

import jax
import jax.numpy as jnp
from jax import lax
from jax.experimental import pallas as pl
from jax.experimental.pallas import tpu as pltpu
from jax.sharding import PartitionSpec as P

MESH = pl.DeviceIdType.MESH
W = 128
G = 8
REP = 8
NSLOT = 5
NB = 4
GB = G // NB
ROWS = 1024
SCALE = 1.0 / math.sqrt(W)
LOG2E = 1.4426950408889634
BF = jnp.bfloat16
F32 = jnp.float32


def dot(a, b, ca, cb):
    return lax.dot_general(a, b, (((ca,), (cb,)), ((), ())), preferred_element_type=F32)


def kernel(
    q_hbm, k_ref, v_ref, do_hbm, l_hbm, doc_ref,
    dq_hbm, dk_hbm, wg_hbm,
    q_vm, do_vm, kv, docx, bias, prob, low_vm, ds_vm, acc, xtx, xrx, ytx, yrx, dvall, lall, lt,
    keep, wtx, wrx, wout, dq_vm, dk_vm,
    in_sem, doc_ss, doc_rs, ky_ss, ky_rs, kx_ss, kx_rs, l_ss, l_rs, px_ss, px_rs, py_ss, py_rs,
    gx_ss, gx_rs, gy_ss, gy_rs, w_ss, w_rs, oy_ss, oy_rs, ox_ss, ox_rs, out_sem,
):
    s = lax.axis_index("section")
    j = lax.axis_index("seq")
    sec = s // 8
    y = j // 2
    xh = j % 2
    mine = ((sec + xh) % 2) * 4 + y
    partner = j + 1 - 2 * xh

    def remote(src, dst, ss, rs, to):
        return pltpu.make_async_remote_copy(
            src_ref=src, dst_ref=dst, send_sem=ss, recv_sem=rs, device_id=to, device_id_type=MESH
        )

    def of_section(sec2):
        return s + (sec2 + sec - 2 * sec * sec2) * (15 - 2 * s)

    def holder(r):
        return of_section((r // 4 + xh) % 2), 2 * (r % 4) + xh

    def rows_of(r):
        return pl.ds(pl.multiple_of(r * ROWS, ROWS), ROWS)

    def heads(b):
        return pl.ds(b * GB, GB)

    q_in = pltpu.make_async_copy(q_hbm, q_vm, in_sem.at[0])
    do_in = pltpu.make_async_copy(do_hbm, do_vm, in_sem.at[1])
    l_own = pltpu.make_async_copy(l_hbm.at[:, rows_of(mine)], lall.at[sec, y], in_sem.at[2])
    q_in.start()
    do_in.start()
    l_own.start()

    barrier = pltpu.get_barrier_semaphore()

    def greet(to):
        pl.semaphore_signal(barrier, inc=1, device_id=to, device_id_type=MESH)

    def greet_own(k, c):
        greet((s, (j + k) % 8))
        return c

    def greet_mirror(k, c):
        greet((15 - s, 2 * k + xh))
        return c

    lax.fori_loop(1, 8, greet_own, 0)
    lax.fori_loop(0, 4, greet_mirror, 0)
    greet((15 - s, partner))

    for g in range(G):
        kv[0, g, 0] = k_ref[:, g * W:(g + 1) * W]
        kv[1, g, 0] = v_ref[:, g * W:(g + 1) * W]
    docx[0] = jnp.broadcast_to(doc_ref[...], (8, W))
    for d in range(1, NSLOT):
        @pl.when(j < d)
        def _():
            kv[:, :, d] = jnp.zeros((2, G, W, W), BF)
            docx[d] = jnp.zeros((8, W), jnp.int32)

    pl.semaphore_wait(barrier, 12)

    def doc_copy(d):
        return remote(docx.at[0], docx.at[d], doc_ss.at[d], doc_rs.at[d], (s, j + d))

    def kv_y(kind, b, n):
        return remote(
            kv.at[kind, heads(b), 0], kv.at[kind, heads(b), 2 * n + 2],
            ky_ss.at[kind, b, n], ky_rs.at[kind, b, n], (s, j + 2 * n + 2),
        )

    def kv_x(kind, b, n):
        return remote(
            kv.at[kind, heads(b), 2 * n + 2 * xh], kv.at[kind, heads(b), 2 * n + 1],
            kx_ss.at[kind, b, n], kx_rs.at[kind, b, n], (s, partner),
        )

    def send_kv(kind, b):
        @pl.when(xh == 0)
        def _():
            kv_x(kind, b, 0).start()

        for n in range(2):
            @pl.when(j + 2 * n + 2 < 8)
            def _():
                kv_y(kind, b, n).start()

    def relay_kv(kind, b):
        for n in range(2):
            @pl.when(j >= 2 * n + 2)
            def _():
                kv_y(kind, b, n).wait_recv()

        for n in range(2):
            @pl.when((j >= 2 * n + 2 * xh) & (n + xh > 0))
            def _():
                kv_x(kind, b, n).start()

    def got_kv(kind, b):
        for n in range(2):
            @pl.when(j >= 2 * n + 1)
            def _():
                kv_x(kind, b, n).wait_recv()

    for d in range(1, NSLOT):
        @pl.when(j + d < 8)
        def _():
            doc_copy(d).start()

    def send_all(b, c):
        send_kv(0, b)
        return c

    lax.fori_loop(0, NB, send_all, 0)

    def peer(k):
        return ((sec + k // 4 + xh) % 2) * 4 + (y + k) % 4

    def l_copy(k):
        r = peer(k)
        return remote(l_hbm.at[:, rows_of(r)], lall.at[sec, y], l_ss.at[k], l_rs.at[k], holder(r))

    def send_l(k, c):
        l_copy(k).start()
        return c

    for d in range(1, NSLOT):
        @pl.when(j >= d)
        def _():
            doc_copy(d).wait_recv()

    row = lax.broadcasted_iota(jnp.int32, (W, W), 0)
    col = lax.broadcasted_iota(jnp.int32, (W, W), 1)
    q_doc = jnp.broadcast_to(docx[0, 0:1], (W, W)).astype(F32)
    for d in range(NSLOT):
        key_doc = jnp.broadcast_to(docx[d, 0:1], (W, W)).astype(F32).T
        seen = (key_doc == q_doc) & (j >= d)
        if d == 0:
            seen = seen & (row <= col)
        bias[d * W:(d + 1) * W] = jnp.where(seen, 0.0, -jnp.inf).astype(F32)

    q_in.wait()
    do_in.wait()

    def two_heads(ref, g, p):
        both = ref[:, pl.ds(pl.multiple_of((g * REP + 2 * p) * W, 2 * W), 2 * W)]
        return jnp.concatenate([both[:, :W], both[:, W:]], axis=0)

    def group_rows(ref, g):
        return jnp.concatenate(
            [ref[:, pl.ds(pl.multiple_of((g * REP + h) * W, W), W)] for h in range(REP)], axis=0
        )

    def part_sums(kind, g, left, right):
        for d in range(NSLOT):
            part = dot(left[d * W:(d + 1) * W], right, 1, 0)
            if d % 2 == 0:
                acc[kind, g, d // 2] = part
            else:
                xtx[kind, g, d // 2] = part.astype(BF)

    def probabilities(g):
        keys = kv.at[0, g]

        def pair(p, c):
            q2 = two_heads(q_vm, g, p)
            t = []
            m = None
            for d in range(NSLOT):
                bd = bias[d * W:(d + 1) * W]
                td = dot(keys[d], q2, 1, 1) * (SCALE * LOG2E) + jnp.concatenate([bd, bd], axis=1)
                t.append(td)
                md = jnp.max(td, axis=0, keepdims=True)
                m = md if m is None else jnp.maximum(m, md)
            total = None
            for d in range(NSLOT):
                t[d] = jnp.exp2(t[d] - m)
                ld = jnp.sum(t[d], axis=0, keepdims=True)
                total = ld if total is None else total + ld
            inv = 1.0 / total
            out = pl.ds(pl.multiple_of(p * 2 * W, 2 * W), 2 * W)
            for d in range(NSLOT):
                pd = t[d] * inv
                prob[g, p, d * W:(d + 1) * W] = pd
                low_vm[d * W:(d + 1) * W, out] = pd.astype(BF)
            return c

        lax.fori_loop(0, REP // 2, pair, 0)
        part_sums(1, g, low_vm, group_rows(do_vm, g))

    def score_grads(g):
        values = kv.at[1, g]

        def pair(p, c):
            o2 = two_heads(do_vm, g, p)
            delta = None
            dps = []
            for d in range(NSLOT):
                dp = dot(values[d], o2, 1, 1)
                dps.append(dp)
                low = prob[g, p, d * W:(d + 1) * W].astype(BF).astype(F32)
                dd = jnp.sum(low * dp, axis=0, keepdims=True)
                delta = dd if delta is None else delta + dd
            out = pl.ds(pl.multiple_of(p * 2 * W, 2 * W), 2 * W)
            for d in range(NSLOT):
                pd = prob[g, p, d * W:(d + 1) * W]
                ds_vm[d * W:(d + 1) * W, out] = (pd * ((dps[d] - delta) * SCALE)).astype(BF)
            return c

        lax.fori_loop(0, REP // 2, pair, 0)
        part_sums(0, g, ds_vm, group_rows(q_vm, g))
        k_t = kv[0, g].reshape(NSLOT * W, W).T
        for h in range(REP):
            dqt = dot(k_t, ds_vm[:, h * W:(h + 1) * W], 1, 0)
            dq_vm[:, pl.ds(pl.multiple_of((g * REP + h) * W, W), W)] = dqt.T.astype(BF)

    def part_x(kind, b, n):
        return remote(
            xtx.at[kind, heads(b), n], xrx.at[kind, heads(b), n],
            px_ss.at[kind, b, n], px_rs.at[kind, b, n], (s, partner),
        )

    def part_y(kind, b, n):
        return remote(
            ytx.at[kind, heads(b), n], yrx.at[kind, heads(b), n],
            py_ss.at[kind, b, n], py_rs.at[kind, b, n], (s, j - 2 * n - 2),
        )

    def send_parts(kind, b):
        for n in range(2):
            @pl.when(j >= 2 * n + 1)
            def _():
                part_x(kind, b, n).start()

    def cross_parts(kind, b):
        for n in range(2):
            @pl.when(partner >= 2 * n + 1)
            def _():
                part_x(kind, b, n).wait_recv()
                for gg in range(GB):
                    g = b * GB + gg
                    acc[kind, g, n + xh] = acc[kind, g, n + xh] + xrx[kind, g, n].astype(F32)

        for n in range(2):
            @pl.when(j >= 2 * n + 2)
            def _():
                ytx[kind, heads(b), n] = acc[kind, heads(b), n + 1].astype(BF)
                part_y(kind, b, n).start()

    def own_sums(kind, b):
        for n in range(2):
            @pl.when(j + 2 * n + 2 < 8)
            def _():
                part_y(kind, b, n).wait_recv()
                for gg in range(GB):
                    g = b * GB + gg
                    acc[kind, g, 0] = acc[kind, g, 0] + yrx[kind, g, n].astype(F32)

    def gather_x(b):
        block = dvall.at[b, sec, y]
        return remote(block, block, gx_ss.at[b], gx_rs.at[b], (15 - s, j))

    def gather_y(b, e):
        blocks = dvall.at[b, :, y]
        to = (s, 2 * ((y + e) % 4) + xh)
        return remote(blocks, blocks, gy_ss.at[b, e], gy_rs.at[b, e], to)

    def value_grads(b):
        own_sums(1, b)
        for gg in range(GB):
            dvall[b, sec, y, :, gg * W:(gg + 1) * W] = acc[1, b * GB + gg, 0].astype(BF)
        gather_x(b).start()

    def key_grads(b):
        own_sums(0, b)
        for gg in range(GB):
            g = b * GB + gg
            dk_vm[:, pl.ds(pl.multiple_of(g * W, W), W)] = acc[0, g, 0].astype(BF)

    def forward(b):
        gather_x(b).wait_recv()
        for e in range(1, 4):
            gather_y(b, e).start()

    def w_copy(b):
        return remote(wtx.at[b], wrx.at[b], w_ss.at[b], w_rs.at[b], (15 - s, partner))

    def turn(k):
        return (y + k) % 4

    def weights(k):
        b = turn(k)

        @pl.when(k == 0)
        def _():
            def wait_gather(b2, c):
                for e in range(1, 4):
                    gather_y(b2, e).wait_recv()
                return c

            lax.fori_loop(0, NB, wait_gather, 0)
            l_own.wait()

            def wait_l(k2, c):
                l_copy(k2).wait_recv()
                return c

            lax.fori_loop(1, 8, wait_l, 0)
            for r in range(ROWS // W):
                la = lall[:, :, :, r * W:(r + 1) * W].reshape(8 * W, W)
                lt[r * W:(r + 1) * W] = la.T

        dv = dvall[b].reshape(8 * W, GB * W)

        def chunk(r, c):
            at = pl.ds(pl.multiple_of(r * 2 * W, 2 * W), 2 * W)
            res = dot(lt[at], dv, 1, 0)
            keep[b, at] = jnp.where(xh == 0, res[:, :W], res[:, W:])
            wtx[b, at] = jnp.where(xh == 0, res[:, W:], res[:, :W]).astype(BF)
            return c

        lax.fori_loop(0, ROWS // (2 * W), chunk, 0)
        w_copy(b).start()

    def column_rows(y2):
        return rows_of(((sec + xh) % 2) * 4 + y2)

    def out_y(k):
        b = turn(k)
        return remote(
            wout.at[b], wg_hbm.at[rows_of(mine)], oy_ss.at[k], oy_rs.at[k], (s, 2 * b + xh)
        )

    def out_own():
        return pltpu.make_async_copy(wout.at[y], wg_hbm.at[rows_of(mine)], out_sem.at[2])

    def hand_own():
        return remote(
            wout.at[y], wg_hbm.at[rows_of(mine)], ox_ss.at[0], ox_rs.at[0], (15 - s, j)
        )

    def hand_on(k):
        at = wg_hbm.at[column_rows((y + 4 - k) % 4)]
        return remote(at, at, ox_ss.at[k], ox_rs.at[k], (15 - s, j))

    def finish(k):
        b = turn(k)
        w_copy(b).wait_recv()
        wout[b] = (keep[b] + wrx[b].astype(F32)).astype(BF)

        @pl.when(k == 0)
        def _():
            out_own().start()
            hand_own().start()

        @pl.when(k > 0)
        def _():
            out_y(k).start()

    def pass_on(k):
        @pl.when(k > 0)
        def _():
            out_y(k).wait_recv()
            hand_on(k).start()

    relay_kv(0, 0)

    def step(i, c):
        def at(first, do, *args):
            @pl.when((i >= first) & (i < first + NB))
            def _():
                do(*args, i - first)

        @pl.when(i < NB - 1)
        def _():
            relay_kv(0, i + 1)

        @pl.when(i < NB)
        def _():
            send_kv(1, i)

        @pl.when((i >= 2) & (i < 6))
        def _():
            lax.fori_loop(jnp.maximum(2 * i - 4, 1), 2 * i - 2, send_l, 0)

        @pl.when((i >= NB - 1) & (i < 2 * NB - 1))
        def _():
            relay_kv(1, i - (NB - 1))

        def first_half(b):
            got_kv(0, b)

            def group(gg, c2):
                probabilities(b * GB + gg)
                return c2

            lax.fori_loop(0, GB, group, 0)
            send_parts(1, b)

        def second_half(b):
            got_kv(1, b)

            def group(gg, c2):
                score_grads(b * GB + gg)
                return c2

            lax.fori_loop(0, GB, group, 0)
            send_parts(0, b)

        at(0, first_half)
        at(1, cross_parts, 1)
        at(2, value_grads)
        at(3, forward)
        at(7, weights)
        at(8, finish)
        at(9, pass_on)
        at(NB, second_half)
        at(NB + 1, cross_parts, 0)
        at(NB + 2, key_grads)
        return c

    lax.fori_loop(0, NB + 9, step, 0)

    dq_out = pltpu.make_async_copy(dq_vm, dq_hbm, out_sem.at[0])
    dk_out = pltpu.make_async_copy(dk_vm, dk_hbm, out_sem.at[1])
    dq_out.start()
    dk_out.start()

    def end_batch(b, c):
        for kind in range(2):
            @pl.when(xh == 0)
            def _():
                kv_x(kind, b, 0).wait_send()

            for n in range(2):
                @pl.when(j + 2 * n + 2 < 8)
                def _():
                    kv_y(kind, b, n).wait_send()

                @pl.when((j >= 2 * n + 2 * xh) & (n + xh > 0))
                def _():
                    kv_x(kind, b, n).wait_send()

                @pl.when(j >= 2 * n + 1)
                def _():
                    part_x(kind, b, n).wait_send()

                @pl.when(j >= 2 * n + 2)
                def _():
                    part_y(kind, b, n).wait_send()

        gather_x(b).wait_send()
        for e in range(1, 4):
            gather_y(b, e).wait_send()
        w_copy(b).wait_send()
        return c

    lax.fori_loop(0, NB, end_batch, 0)
    for d in range(1, NSLOT):
        @pl.when(j + d < 8)
        def _():
            doc_copy(d).wait_send()

    def end_l(k, c):
        l_copy(k).wait_send()
        return c

    lax.fori_loop(1, 8, end_l, 0)
    out_own().wait()
    hand_own().wait()

    def end_out(k, c):
        out_y(k).wait_send()
        hand_on(k).wait()
        return c

    lax.fori_loop(1, 4, end_out, 0)
    dq_out.wait()
    dk_out.wait()


def local(queries, key_states, section_value_states, out_grad, layer_input, doc_segments):
    hbm = pl.BlockSpec(memory_space=pl.ANY)
    vmem = pl.BlockSpec(memory_space=pltpu.VMEM)
    dma = pltpu.SemaphoreType.DMA
    dq, dk, wg = pl.pallas_call(
        kernel,
        out_shape=(
            jax.ShapeDtypeStruct((W, 8192), BF),
            jax.ShapeDtypeStruct((W, G * W), BF),
            jax.ShapeDtypeStruct((8192, W), BF),
        ),
        in_specs=[hbm, vmem, vmem, hbm, hbm, vmem],
        out_specs=(hbm, hbm, hbm),
        scratch_shapes=[
            pltpu.VMEM((W, 8192), BF),
            pltpu.VMEM((W, 8192), BF),
            pltpu.VMEM((2, G, NSLOT, W, W), BF),
            pltpu.VMEM((NSLOT, 8, W), jnp.int32),
            pltpu.VMEM((NSLOT * W, W), F32),
            pltpu.VMEM((G, REP // 2, NSLOT * W, 2 * W), F32),
            pltpu.VMEM((NSLOT * W, REP * W), BF),
            pltpu.VMEM((NSLOT * W, REP * W), BF),
            pltpu.VMEM((2, G, 3, W, W), F32),
            pltpu.VMEM((2, G, 2, W, W), BF),
            pltpu.VMEM((2, G, 2, W, W), BF),
            pltpu.VMEM((2, G, 2, W, W), BF),
            pltpu.VMEM((2, G, 2, W, W), BF),
            pltpu.VMEM((NB, 2, 4, W, GB * W), BF),
            pltpu.VMEM((2, 4, W, ROWS), BF),
            pltpu.VMEM((ROWS, 8 * W), BF),
            pltpu.VMEM((NB, ROWS, W), F32),
            pltpu.VMEM((NB, ROWS, W), BF),
            pltpu.VMEM((NB, ROWS, W), BF),
            pltpu.VMEM((NB, ROWS, W), BF),
            pltpu.VMEM((W, 8192), BF),
            pltpu.VMEM((W, G * W), BF),
            dma((3,)),
            dma((NSLOT,)), dma((NSLOT,)),
            dma((2, NB, 2)), dma((2, NB, 2)),
            dma((2, NB, 2)), dma((2, NB, 2)),
            dma((8,)), dma((8,)),
            dma((2, NB, 2)), dma((2, NB, 2)),
            dma((2, NB, 2)), dma((2, NB, 2)),
            dma((NB,)), dma((NB,)),
            dma((NB, 4)), dma((NB, 4)),
            dma((NB,)), dma((NB,)),
            dma((4,)), dma((4,)),
            dma((4,)), dma((4,)),
            dma((3,)),
        ],
        compiler_params=pltpu.CompilerParams(
            collective_id=0, has_side_effects=True, vmem_limit_bytes=58 << 20
        ),
        cost_estimate=pl.CostEstimate(
            flops=10_000_000_000, bytes_accessed=12_000_000, transcendentals=5_000_000
        ),
        name="attention_weight_grad",
    )(
        queries[0], key_states[0], section_value_states[0], out_grad[0], layer_input[0],
        doc_segments,
    )
    return dq[None], dk[None], wg[None]


def solution(mesh):
    rows = P("section", "seq", None)
    return jax.shard_map(
        local,
        mesh=mesh,
        in_specs=(rows, rows, rows, rows, rows, P("section", "seq")),
        out_specs=(rows, rows, P("section", None, "seq")),
        check_vma=False,
    )
```
